32 devices in a mesh: seq: 8 (over z, core), blk: 4 (over y, x).
Axes of the slice: x: 2, y: 2, z: 4, core: 2. Of those that a mesh axis runs over, the one named last changes fastest.
Arguments:
- tokens: bfloat16 [8192, 8192], P('seq', 'blk'), may hold values from -6 to 6
- right_factor: bfloat16 [64, 128, 128], P('blk', 'seq'), may hold values from -0.5 to 0.5
- left_factor: bfloat16 [128, 64, 64], P('blk', 'seq'), may hold values from -0.75 to 0.75
- target: bfloat16 [8192, 8192], P('seq', 'blk'), may hold values from -4 to 4
Outputs:
- student: bfloat16 [8192, 8192], P('seq', 'blk')
- right_grad: float32 [64, 128, 128], P('blk', 'seq')
- left_grad: float32 [128, 64, 64], P('blk', 'seq')
The draws below stay inside these ranges and needn't reach their ends.
All inputs are finite; a program needn't handle non-finite values.
Results may differ from the reference program's by a relative error of at most 0.017.
Values may be sent and summed in bfloat16 or wider, within the bound.
A program may use at most 64 MiB of HBM per device.

```python
import jax
import jax.numpy as jnp

D = 8192
BLOCK = 128
NBLOCKS = 64
TOKENS = 8192


def levels(own_key, dims, split, smallest, largest):
    level = 1.0
    for position, parts in split:
        heights = jax.random.uniform(jax.random.fold_in(jax.random.fold_in(own_key, 6), position), (parts,), jnp.float32, smallest / len(split), largest / len(split))
        level = level * jnp.repeat(jnp.exp(heights), dims[position] // parts).reshape((-1,) + (1,) * (len(dims) - 1 - position))
    return level


def noise(stream_key, extent, scale, bound, shards=(), dtype=jnp.bfloat16):
    drawn = scale * jax.random.normal(stream_key, extent, jnp.float32)
    if shards:
        drawn = drawn * levels(stream_key, extent, shards, -0.22, 0.18)
    return jnp.clip(drawn, -bound, bound).astype(dtype)


def setup_inputs(seed: int = 0) -> dict:
    keys = jax.random.split(jax.random.key(seed), 5)
    return {
        "tokens": noise(keys[0], (TOKENS, D), 1.0, 6.0, ((0, 8), (1, 4))),
        "right_factor": noise(keys[1], (NBLOCKS, BLOCK, BLOCK), BLOCK ** -0.5, 0.5, ((0, 4), (1, 8))),
        "left_factor": noise(keys[2], (BLOCK, NBLOCKS, NBLOCKS), NBLOCKS ** -0.5, 0.75, ((0, 4), (1, 8))),
        "target": noise(keys[3], (TOKENS, D), 0.5, 4.0, ((0, 8), (1, 4))),
    }


def gelu_tanh(values):
    return jax.nn.gelu(values, approximate=True)

def reference(tokens, right_factor, left_factor, target):
    count = tokens.shape[0]
    scale = 1.0 / jnp.sqrt(jnp.float32(count))
    inputs = tokens.reshape(count, NBLOCKS, BLOCK).astype(jnp.float32)
    mixed = jnp.einsum('tki,kci->tkc', inputs, right_factor.astype(jnp.float32)).astype(jnp.bfloat16)
    turned = jnp.transpose(mixed, (0, 2, 1)).astype(jnp.float32)
    left_wide = left_factor.astype(jnp.float32)
    pre = jnp.einsum('tck,cmk->tcm', turned, left_wide)
    act, back = jax.vjp(gelu_tanh, pre)
    student = act.reshape(count, D).astype(jnp.bfloat16)
    residual = (act - target.reshape(count, BLOCK, NBLOCKS).astype(jnp.float32)) * scale
    pre_grad = back(residual)[0].astype(jnp.bfloat16).astype(jnp.float32)
    turned_grad = jnp.einsum('tcm,cmk->tck', pre_grad, left_wide).astype(jnp.bfloat16).astype(jnp.float32)
    left_grad = jnp.einsum('tcm,tck->cmk', pre_grad, turned)
    right_grad = jnp.einsum('tck,tki->kci', turned_grad, inputs)
    return (student, right_grad, left_grad)
```

```python
import functools
import math

import jax
import jax.numpy as jnp
from jax import lax
from jax.experimental import pallas as pl
from jax.experimental.pallas import tpu as pltpu
from jax.sharding import PartitionSpec as P

MESH = pl.DeviceIdType.MESH
F32 = jnp.float32
BF16 = jnp.bfloat16
C0 = math.sqrt(2.0 / math.pi)
NT = (((1,), (1,)), ((), ()))
NN = (((1,), (0,)), ((), ()))


def dot(a, b, dims):
    return lax.dot_general(a, b, dims, preferred_element_type=F32)


def partner(b, d, size):
    step, out = 1, b
    while step < size:
        if (d // step) % 2:
            out = out + step * (1 - 2 * ((b // step) % 2))
        step *= 2
    return out


def stack(parts):
    if parts[0].shape[0] % 16:
        return jnp.concatenate([v.astype(F32) for v in parts], axis=0).astype(BF16)
    return jnp.concatenate(parts, axis=0)


def eye(n):
    return (
        lax.broadcasted_iota(jnp.int32, (n, n), 0) == lax.broadcasted_iota(jnp.int32, (n, n), 1)
    ).astype(F32).astype(BF16)


def kernel(
    cfg, x_hbm, f_hbm, t_hbm, st_hbm, rg_out, lg_out,
    xv, tv, stv, snd, recv, bsnd, brecv, fm, ft,
    gat, gf, rfull, lc, wb, wt, rg, lg, lga, idt,
    pbr, sibr, zsr, zrr, pbl, sibl, zsl, zrl,
    sx, sto, sf, gs, gr, fs, fr,
    as_, ar, al, bs, br, bl,
    rs1, rr1, rs2, rr2, ls1, lr1, ls2, lr2,
):
    S, B, NC, tc, kl, cl, nb, w, r, lr = cfg
    Q = S // 2
    H = tc // 128
    s = lax.axis_index("seq")
    b = lax.axis_index("blk")
    q, core = s // 2, s % 2
    scale = 1.0 / math.sqrt(float(S * NC * tc))
    rrows, lrows = kl * r, (cl // 2) * lr
    sib = (s + 1 - 2 * core, b)
    zpeers = [((((q + o) % Q) * 2 + core), b) for o in range(1, Q)]
    bids = [partner(b, d, B) for d in range(B - 1, 0, -1)]
    bpeers = [(s, i) for i in bids]

    def xload(j):
        return pltpu.make_async_copy(x_hbm.at[pl.ds(pl.multiple_of(j * tc, tc), tc)], xv.at[j], sx.at[0, j])

    def tload(j):
        return pltpu.make_async_copy(t_hbm.at[pl.ds(pl.multiple_of(j * tc, tc), tc)], tv.at[j], sx.at[1, j])

    def stout(j):
        return pltpu.make_async_copy(stv.at[j], st_hbm.at[pl.ds(pl.multiple_of(j * tc, tc), tc)], sto.at[j])

    own = pltpu.make_async_copy(f_hbm, gat.at[s], sf)
    own.start()
    for j in range(NC):
        xload(j).start()
    for j in range(NC):
        tload(j).start()

    barrier = pltpu.get_barrier_semaphore()
    for peer in [sib] + zpeers + bpeers:
        pl.semaphore_signal(barrier, inc=1, device_id=peer, device_id_type=MESH)
    pl.semaphore_wait(barrier, 1 + len(zpeers) + len(bpeers))

    own.wait()
    gsend = [
        pltpu.make_async_remote_copy(
            gat.at[s], gat.at[s], gs.at[o], gr.at[o], device_id=zpeers[o], device_id_type=MESH)
        for o in range(Q - 1)
    ]
    for c in gsend:
        c.start()

    def fwd_copy(o):
        src = ((q - o + Q) % Q) * 2 + core
        return pltpu.make_async_remote_copy(
            gat.at[src], gat.at[src], fs.at[o], fr.at[o], device_id=sib, device_id_type=MESH)

    fsend = [fwd_copy(o) for o in range(Q)]
    fsend[0].start()
    idt[...] = eye(tc)
    rg[...] = jnp.zeros_like(rg)
    lg[...] = jnp.zeros_like(lg)
    for o in range(1, Q):
        gsend[o - 1].wait_recv()
        fsend[o].start()
    for o in range(Q):
        fsend[o].wait_recv()

    for i in range(S):
        gf[i] = gat[i, :rrows, :].astype(F32).reshape(kl, r, w)

    def rbuild(k, _):
        rfull[k] = jnp.concatenate([gf[i, k] for i in range(S)], axis=0).astype(BF16)
        return 0

    lax.fori_loop(0, kl, rbuild, 0)

    def a_copy(j, d):
        return pltpu.make_async_remote_copy(
            snd.at[j, pl.ds(pl.multiple_of(bids[d] * cl, cl), cl)], recv.at[j, b],
            as_.at[j, d], ar.at[j, d], device_id=bpeers[d], device_id_type=MESH)

    def a_local(j):
        return pltpu.make_async_copy(
            snd.at[j, pl.ds(pl.multiple_of(b * cl, cl), cl)], recv.at[j, b], al.at[j])

    def forward(j, _):
        xload(j).wait()

        def mm(k, _):
            res = dot(rfull[k], xv[j, :, pl.ds(pl.multiple_of(k * w, w), w)], NT)
            for h in range(H):
                fm[h, pl.ds(pl.multiple_of(k * w, w), w), :] = res[:, h * 128:(h + 1) * 128]
            return 0

        lax.fori_loop(0, kl, mm, 0)

        def turn(g, _):
            for u in range(8):
                c = g * 8 + u
                for h in range(H):
                    snd[j, c, :, h * 128:(h + 1) * 128] = fm[h, pl.ds(c, kl, stride=w), :].astype(BF16)
            return 0

        lax.fori_loop(0, w // 8, turn, 0)
        for d in range(B - 1):
            a_copy(j, d).start()
        a_local(j).start()
        return 0

    lax.fori_loop(0, NC, forward, 0)

    gl = fm.at[0]
    lcols = lax.broadcasted_iota(jnp.int32, (nb, 128), 1)
    for i in range(S):
        gl[i * lrows:(i + 1) * lrows, :] = gat[i, rrows:rrows + lrows, :].astype(F32)
    e128 = eye(128)

    def lbuild(p, _):
        for m in range(lr):
            lc[pl.ds(m, S, stride=lr), :] = gl[pl.ds(p * lr + m, S, stride=lrows), :]
        v = lc[...]
        both = jnp.concatenate(
            [jnp.where(lcols < nb, v, 0.0), jnp.where(lcols >= nb, v, 0.0)], axis=0).astype(BF16)
        wb[p] = both
        wt[p] = dot(e128, both, NT).astype(BF16)
        return 0

    lax.fori_loop(0, cl // 2, lbuild, 0)

    def b_copy(j, d):
        return pltpu.make_async_remote_copy(
            bsnd.at[j, pl.ds(pl.multiple_of(bids[d] * kl, kl), kl)], brecv.at[j, b],
            bs.at[j, d], br.at[j, d], device_id=bpeers[d], device_id_type=MESH)

    def b_local(j):
        return pltpu.make_async_copy(
            bsnd.at[j, pl.ds(pl.multiple_of(b * kl, kl), kl)], brecv.at[j, b], bl.at[j])

    def middle(j, _):
        tload(j).wait()
        a_local(j).wait()
        for d in range(B - 1):
            a_copy(j, d).wait_recv()

        def pair(p, _):
            tp = stack([recv[j, a, 2 * p + c] for c in range(2) for a in range(B)])
            cols = pl.ds(pl.multiple_of(p * 128, 128), 128)
            v = dot(wb[p], tp, NN)
            tgt = dot(idt[:128, :128], tv[j, :, cols], NT)
            v2 = v * v
            th = jnp.tanh(v * (C0 + (C0 * 0.044715) * v2))
            half = 0.5 + 0.5 * th
            act = v * half
            deriv = half + 0.5 * v * (1.0 - th * th) * (C0 + (3.0 * 0.044715 * C0) * v2)
            pg = (((act - tgt) * scale) * deriv).astype(BF16)
            stv[j, :, cols] = dot(idt[...], act.astype(BF16), NT).astype(BF16)
            tg = dot(wt[p], pg, NN)
            for h in range(H):
                ft[h, pl.ds(pl.multiple_of(p * 128, 128), 128), :] = tg[:, h * 128:(h + 1) * 128]
            full = dot(pg, tp, NT)
            rows = pl.ds(pl.multiple_of(p * nb, nb), nb)
            lg[rows, :] += jnp.where(lcols < nb, full[:nb], full[nb:])
            return 0

        lax.fori_loop(0, cl // 2, pair, 0)

        def turn(g, _):
            for u in range(4):
                k = g * 4 + u
                for h in range(H):
                    bsnd[j, k, :, h * 128:(h + 1) * 128] = ft[h, pl.ds(k, cl, stride=nb), :].astype(BF16)
            return 0

        lax.fori_loop(0, nb // 4, turn, 0)
        for d in range(B - 1):
            b_copy(j, d).start()
        b_local(j).start()
        stout(j).start()
        return 0

    lax.fori_loop(0, NC, middle, 0)

    l1 = pltpu.make_async_remote_copy(
        pbl.at[1 - core], sibl, ls1, lr1, device_id=sib, device_id_type=MESH)
    for i in range(S):
        for m in range(lr):
            lga[pl.ds(m, cl // 2, stride=lr), :] = lg[pl.ds(i * lr + m, cl // 2, stride=nb), :]
        pbl[i % 2, i // 2] = lga[...].astype(BF16)
    l1.start()

    def right(j, _):
        b_local(j).wait()
        for d in range(B - 1):
            b_copy(j, d).wait_recv()

        def one(k, _):
            mg = stack([brecv[j, a, k] for a in range(B)])
            rg[k] += dot(mg, xv[j, :, pl.ds(pl.multiple_of(k * w, w), w)], NN)
            return 0

        lax.fori_loop(0, kl, one, 0)
        return 0

    def second(pb, sibv, zs, zr, ss, rs):
        for i in range(Q):
            zs[i] = (pb[core, i].astype(F32) + sibv[i].astype(F32)).astype(BF16)
        zr[q] = zs[q]
        copies = [
            pltpu.make_async_remote_copy(
                zs.at[(q + o + 1) % Q], zr.at[q], ss.at[o], rs.at[o],
                device_id=zpeers[o], device_id_type=MESH)
            for o in range(Q - 1)
        ]
        for c in copies:
            c.start()
        return copies

    def total(zr):
        acc = zr[0].astype(F32)
        for i in range(1, Q):
            acc = acc + zr[i].astype(F32)
        return acc

    right(0, 0)
    l1.wait_recv()
    l2 = second(pbl, sibl, zsl, zrl, ls2, lr2)
    lax.fori_loop(1, NC, right, 0)

    for i in range(S):
        pbr[i % 2, i // 2] = rg[:, i * r:(i + 1) * r, :].reshape(rrows, w).astype(BF16)
    r1 = pltpu.make_async_remote_copy(
        pbr.at[1 - core], sibr, rs1, rr1, device_id=sib, device_id_type=MESH)
    r1.start()
    for c in l2:
        c.wait_recv()
    lg_out[...] = total(zrl)
    r1.wait_recv()
    r2 = second(pbr, sibr, zsr, zrr, rs2, rr2)
    for c in gsend + fsend + [l1, r1] + l2:
        c.wait_send()

    def drain(j, _):
        for d in range(B - 1):
            a_copy(j, d).wait_send()
            b_copy(j, d).wait_send()
        stout(j).wait()
        return 0

    lax.fori_loop(0, NC, drain, 0)
    for c in r2:
        c.wait_recv()
    rg_out[...] = total(zrr)
    for c in r2:
        c.wait_send()


def shards(S, B, tokens, right_factor, left_factor, target):
    rows, cols = tokens.shape
    kl, r, w = right_factor.shape
    cl, lr, nb = left_factor.shape
    Q = S // 2
    NC = 4
    tc = rows // NC
    H = tc // 128
    rrows, lrows = kl * r, (cl // 2) * lr
    folded = left_factor.reshape(cl // 2, 2, lr, nb).transpose(0, 2, 1, 3).reshape(lrows, 2 * nb)
    factors = jnp.concatenate([right_factor.reshape(rrows, w), folded], axis=0)
    cfg = (S, B, NC, tc, kl, cl, nb, w, r, lr)
    V = pltpu.VMEM
    D = pltpu.SemaphoreType.DMA
    student, right, left = pl.pallas_call(
        functools.partial(kernel, cfg),
        out_shape=(
            jax.ShapeDtypeStruct((rows, cols), BF16),
            jax.ShapeDtypeStruct((rrows, w), F32),
            jax.ShapeDtypeStruct((lrows, 2 * nb), F32),
        ),
        in_specs=[pl.BlockSpec(memory_space=pl.ANY)] * 3,
        out_specs=(
            pl.BlockSpec(memory_space=pl.ANY),
            pl.BlockSpec(memory_space=V),
            pl.BlockSpec(memory_space=V),
        ),
        scratch_shapes=[
            V((NC, tc, cols), BF16), V((NC, tc, cols), BF16), V((NC, tc, cols), BF16),
            V((NC, w, kl, tc), BF16), V((NC, B, cl, kl, tc), BF16),
            V((NC, nb, cl, tc), BF16), V((NC, B, kl, cl, tc), BF16),
            V((H, kl * w, 128), F32), V((H, cl * nb, 128), F32),
            V((S, rrows + lrows, w), BF16), V((S, kl, r, w), F32), V((kl, w, w), BF16),
            V((nb, 128), F32), V((cl // 2, 128, 128), BF16), V((cl // 2, 128, 128), BF16),
            V((kl, w, w), F32), V((cl // 2 * nb, 128), F32), V((lrows, 128), F32), V((tc, tc), BF16),
            V((2, Q, rrows, w), BF16), V((Q, rrows, w), BF16), V((Q, rrows, w), BF16), V((Q, rrows, w), BF16),
            V((2, Q, lrows, w), BF16), V((Q, lrows, w), BF16), V((Q, lrows, w), BF16), V((Q, lrows, w), BF16),
            D((2, NC)), D((NC,)), D, D((Q - 1,)), D((Q - 1,)), D((Q,)), D((Q,)),
            D((NC, B - 1)), D((NC, B - 1)), D((NC,)), D((NC, B - 1)), D((NC, B - 1)), D((NC,)),
            D, D, D((Q - 1,)), D((Q - 1,)), D, D, D((Q - 1,)), D((Q - 1,)),
        ],
        compiler_params=pltpu.CompilerParams(
            collective_id=0, has_side_effects=True, vmem_limit_bytes=56 * 1024 * 1024),
        cost_estimate=pl.CostEstimate(
            flops=4 * 1024 * 1024 * 1024, bytes_accessed=3 * rows * cols * 2, transcendentals=rows * cols),
    )(tokens, factors, target)
    left = left.reshape(cl // 2, lr, 2, nb).transpose(0, 2, 1, 3).reshape(cl, lr, nb)
    return student, right.reshape(kl, r, w), left


def solution(mesh):
    return jax.shard_map(
        functools.partial(shards, mesh.shape["seq"], mesh.shape["blk"]),
        mesh=mesh,
        in_specs=(P("seq", "blk"), P("blk", "seq", None), P("blk", "seq", None), P("seq", "blk")),
        out_specs=(P("seq", "blk"), P("blk", "seq", None), P("blk", "seq", None)),
        check_vma=False,
    )
```

```python
import functools
import math

import jax
import jax.numpy as jnp
from jax import lax
from jax.experimental import pallas as pl
from jax.experimental.pallas import tpu as pltpu
from jax.sharding import PartitionSpec as P

MESH = pl.DeviceIdType.MESH
F32 = jnp.float32
BF16 = jnp.bfloat16
C0 = math.sqrt(2.0 / math.pi)
NT = (((1,), (1,)), ((), ()))
NN = (((1,), (0,)), ((), ()))


def dot(a, b, dims):
    return lax.dot_general(a, b, dims, preferred_element_type=F32)


def partner(b, d, size):
    step, out = 1, b
    while step < size:
        if (d // step) % 2:
            out = out + step * (1 - 2 * ((b // step) % 2))
        step *= 2
    return out


def stack(parts):
    if parts[0].shape[0] % 16:
        return jnp.concatenate([v.astype(F32) for v in parts], axis=0).astype(BF16)
    return jnp.concatenate(parts, axis=0)


def eye(n):
    return (
        lax.broadcasted_iota(jnp.int32, (n, n), 0) == lax.broadcasted_iota(jnp.int32, (n, n), 1)
    ).astype(F32).astype(BF16)


def kernel(
    cfg, x_hbm, r_hbm, l_ref, t_hbm, st_hbm, rg_out, lg_out,
    xv, tv, stv, snd, recv, bsnd, brecv, fm, ft,
    gat, gatl, lfold, gf, rfull, lc, wb, wt, rg, lg, lga, idt,
    pbr, sibr, zsr, zrr, pbl, sibl, zsl, zrl,
    sx, sto, sf, gs, gr, fs, fr, hs, hr, is_, ir,
    as_, ar, al, bs, br, bl,
    rs1, rr1, rs2, rr2, ls1, lr1, ls2, lr2,
):
    S, B, NC, tc, kl, cl, nb, w, r, lr = cfg
    Q = S // 2
    H = tc // 128
    s = lax.axis_index("seq")
    b = lax.axis_index("blk")
    q, core = s // 2, s % 2
    scale = 1.0 / math.sqrt(float(S * NC * tc))
    rrows, lrows = kl * r, (cl // 2) * lr
    sib = (s + 1 - 2 * core, b)
    zpeers = [((((q + o) % Q) * 2 + core), b) for o in range(1, Q)]
    bids = [partner(b, d, B) for d in range(B - 1, 0, -1)]
    bpeers = [(s, i) for i in bids]

    def xload(j):
        return pltpu.make_async_copy(x_hbm.at[pl.ds(pl.multiple_of(j * tc, tc), tc)], xv.at[j], sx.at[0, j])

    def tload(j):
        return pltpu.make_async_copy(t_hbm.at[pl.ds(pl.multiple_of(j * tc, tc), tc)], tv.at[j], sx.at[1, j])

    def stout(j):
        return pltpu.make_async_copy(stv.at[j], st_hbm.at[pl.ds(pl.multiple_of(j * tc, tc), tc)], sto.at[j])

    own = pltpu.make_async_copy(r_hbm, gat.at[s], sf)
    own.start()
    for j in range(NC):
        xload(j).start()

    barrier = pltpu.get_barrier_semaphore()
    for peer in [sib] + zpeers + bpeers:
        pl.semaphore_signal(barrier, inc=1, device_id=peer, device_id_type=MESH)
    pl.semaphore_wait(barrier, 1 + len(zpeers) + len(bpeers))

    def spread(first, buf, ss, rs):
        return [
            pltpu.make_async_remote_copy(
                first, buf.at[s], ss.at[o], rs.at[o], device_id=zpeers[o], device_id_type=MESH)
            for o in range(Q - 1)
        ]

    def pass_on(first, buf, ss, rs):
        out = []
        for o in range(Q):
            src = ((q - o + Q) % Q) * 2 + core
            out.append(pltpu.make_async_remote_copy(
                buf.at[src] if o else first, buf.at[src], ss.at[o], rs.at[o],
                device_id=sib, device_id_type=MESH))
        return out

    gsend = spread(r_hbm, gat, gs, gr)
    fsend = pass_on(r_hbm, gat, fs, fr)
    for c in gsend:
        c.start()
    fsend[0].start()
    for j in range(NC):
        tload(j).start()
    idt[...] = eye(tc)
    rg[...] = jnp.zeros_like(rg)
    lg[...] = jnp.zeros_like(lg)
    for p in range(cl // 2):
        lfold[p * lr:(p + 1) * lr, :] = jnp.concatenate(
            [l_ref[2 * p].astype(F32), l_ref[2 * p + 1].astype(F32)], axis=1)
    gatl[s] = lfold[...].astype(BF16)
    own.wait()
    for o in range(1, Q):
        gsend[o - 1].wait_recv()
        fsend[o].start()
    hsend = spread(gatl.at[s], gatl, hs, hr)
    isend = pass_on(gatl.at[s], gatl, is_, ir)
    for c in hsend:
        c.start()
    isend[0].start()
    for o in range(Q):
        fsend[o].wait_recv()

    for i in range(S):
        gf[i] = gat[i].astype(F32).reshape(kl, r, w)

    def rbuild(k, _):
        rfull[k] = jnp.concatenate([gf[i, k] for i in range(S)], axis=0).astype(BF16)
        return 0

    lax.fori_loop(0, kl, rbuild, 0)

    def a_copy(j, d):
        return pltpu.make_async_remote_copy(
            snd.at[j, pl.ds(pl.multiple_of(bids[d] * cl, cl), cl)], recv.at[j, b],
            as_.at[j, d], ar.at[j, d], device_id=bpeers[d], device_id_type=MESH)

    def a_local(j):
        return pltpu.make_async_copy(
            snd.at[j, pl.ds(pl.multiple_of(b * cl, cl), cl)], recv.at[j, b], al.at[j])

    def forward(j, _):
        xload(j).wait()

        def mm(k, _):
            res = dot(rfull[k], xv[j, :, pl.ds(pl.multiple_of(k * w, w), w)], NT)
            for h in range(H):
                fm[h, pl.ds(pl.multiple_of(k * w, w), w), :] = res[:, h * 128:(h + 1) * 128]
            return 0

        lax.fori_loop(0, kl, mm, 0)

        def turn(g, _):
            for u in range(8):
                c = g * 8 + u
                for h in range(H):
                    snd[j, c, :, h * 128:(h + 1) * 128] = fm[h, pl.ds(c, kl, stride=w), :].astype(BF16)
            return 0

        lax.fori_loop(0, w // 8, turn, 0)
        for d in range(B - 1):
            a_copy(j, d).start()
        a_local(j).start()
        return 0

    lax.fori_loop(0, NC, forward, 0)

    for o in range(1, Q):
        hsend[o - 1].wait_recv()
        isend[o].start()
    for o in range(Q):
        isend[o].wait_recv()

    gl = fm.at[0]
    lcols = lax.broadcasted_iota(jnp.int32, (nb, 128), 1)
    for i in range(S):
        gl[i * lrows:(i + 1) * lrows, :] = gatl[i].astype(F32)
    e128 = idt[:128, :128]

    def lbuild(p, _):
        for m in range(lr):
            lc[pl.ds(m, S, stride=lr), :] = gl[pl.ds(p * lr + m, S, stride=lrows), :]
        v = lc[...]
        both = jnp.concatenate(
            [jnp.where(lcols < nb, v, 0.0), jnp.where(lcols >= nb, v, 0.0)], axis=0).astype(BF16)
        wb[p] = both
        wt[p] = dot(e128, both, NT).astype(BF16)
        return 0

    lax.fori_loop(0, cl // 2, lbuild, 0)

    def b_copy(j, d):
        return pltpu.make_async_remote_copy(
            bsnd.at[j, pl.ds(pl.multiple_of(bids[d] * kl, kl), kl)], brecv.at[j, b],
            bs.at[j, d], br.at[j, d], device_id=bpeers[d], device_id_type=MESH)

    def b_local(j):
        return pltpu.make_async_copy(
            bsnd.at[j, pl.ds(pl.multiple_of(b * kl, kl), kl)], brecv.at[j, b], bl.at[j])

    def middle(j, _):
        tload(j).wait()
        a_local(j).wait()
        for d in range(B - 1):
            a_copy(j, d).wait_recv()

        def pair(p, _):
            tp = stack([recv[j, a, 2 * p + c] for c in range(2) for a in range(B)])
            cols = pl.ds(pl.multiple_of(p * 128, 128), 128)
            v = dot(wb[p], tp, NN)
            tgt = dot(e128, tv[j, :, cols], NT)
            v2 = v * v
            th = jnp.tanh(v * (C0 + (C0 * 0.044715) * v2))
            half = 0.5 + 0.5 * th
            act = v * half
            deriv = half + 0.5 * v * (1.0 - th * th) * (C0 + (3.0 * 0.044715 * C0) * v2)
            pg = (((act - tgt) * scale) * deriv).astype(BF16)
            stv[j, :, cols] = dot(idt[...], act.astype(BF16), NT).astype(BF16)
            tg = dot(wt[p], pg, NN)
            for h in range(H):
                ft[h, pl.ds(pl.multiple_of(p * 128, 128), 128), :] = tg[:, h * 128:(h + 1) * 128]
            full = dot(pg, tp, NT)
            rows = pl.ds(pl.multiple_of(p * nb, nb), nb)
            lg[rows, :] += jnp.where(lcols < nb, full[:nb], full[nb:])
            return 0

        lax.fori_loop(0, cl // 2, pair, 0)

        def turn(g, _):
            for u in range(4):
                k = g * 4 + u
                for h in range(H):
                    bsnd[j, k, :, h * 128:(h + 1) * 128] = ft[h, pl.ds(k, cl, stride=nb), :].astype(BF16)
            return 0

        lax.fori_loop(0, nb // 4, turn, 0)
        for d in range(B - 1):
            b_copy(j, d).start()
        b_local(j).start()
        stout(j).start()
        return 0

    lax.fori_loop(0, NC, middle, 0)

    l1 = pltpu.make_async_remote_copy(
        pbl.at[1 - core], sibl, ls1, lr1, device_id=sib, device_id_type=MESH)
    for i in range(S):
        for m in range(lr):
            lga[pl.ds(m, cl // 2, stride=lr), :] = lg[pl.ds(i * lr + m, cl // 2, stride=nb), :]
        pbl[i % 2, i // 2] = lga[...].astype(BF16)
    l1.start()

    def right(j, _):
        b_local(j).wait()
        for d in range(B - 1):
            b_copy(j, d).wait_recv()

        def one(k, _):
            mg = stack([brecv[j, a, k] for a in range(B)])
            rg[k] += dot(mg, xv[j, :, pl.ds(pl.multiple_of(k * w, w), w)], NN)
            return 0

        lax.fori_loop(0, kl, one, 0)
        return 0

    def second(pb, sibv, zs, zr, ss, rs):
        for i in range(Q):
            zs[i] = (pb[core, i].astype(F32) + sibv[i].astype(F32)).astype(BF16)
        zr[q] = zs[q]
        copies = [
            pltpu.make_async_remote_copy(
                zs.at[(q + o + 1) % Q], zr.at[q], ss.at[o], rs.at[o],
                device_id=zpeers[o], device_id_type=MESH)
            for o in range(Q - 1)
        ]
        for c in copies:
            c.start()
        return copies

    def total(zr):
        acc = zr[0].astype(F32)
        for i in range(1, Q):
            acc = acc + zr[i].astype(F32)
        return acc

    right(0, 0)
    l1.wait_recv()
    l2 = second(pbl, sibl, zsl, zrl, ls2, lr2)
    lax.fori_loop(1, NC, right, 0)

    for i in range(S):
        pbr[i % 2, i // 2] = rg[:, i * r:(i + 1) * r, :].reshape(rrows, w).astype(BF16)
    r1 = pltpu.make_async_remote_copy(
        pbr.at[1 - core], sibr, rs1, rr1, device_id=sib, device_id_type=MESH)
    r1.start()
    for c in l2:
        c.wait_recv()
    lg_out[...] = total(zrl)
    r1.wait_recv()
    r2 = second(pbr, sibr, zsr, zrr, rs2, rr2)
    for c in gsend + fsend + hsend + isend + [l1, r1] + l2:
        c.wait_send()

    def drain(j, _):
        for d in range(B - 1):
            a_copy(j, d).wait_send()
            b_copy(j, d).wait_send()
        stout(j).wait()
        return 0

    lax.fori_loop(0, NC, drain, 0)
    for c in r2:
        c.wait_recv()
    rg_out[...] = total(zrr)
    for c in r2:
        c.wait_send()


def finish(st_ref, rg_ref, lg_ref, st_out, rg_out, lg_out):
    st_out[...] = st_ref[...]

    @pl.when(pl.program_id(0) == 0)
    def _():
        rg_out[...] = rg_ref[...].reshape(rg_out.shape)
        cl, lr, nb = lg_out.shape
        for p in range(cl // 2):
            v = lg_ref[p * lr:(p + 1) * lr, :]
            lg_out[2 * p] = v[:, :nb]
            lg_out[2 * p + 1] = v[:, nb:]


def shards(S, B, tokens, right_factor, left_factor, target):
    rows, cols = tokens.shape
    kl, r, w = right_factor.shape
    cl, lr, nb = left_factor.shape
    Q = S // 2
    NC = 8
    tc = rows // NC
    H = tc // 128
    rrows, lrows = kl * r, (cl // 2) * lr
    cfg = (S, B, NC, tc, kl, cl, nb, w, r, lr)
    V = pltpu.VMEM
    D = pltpu.SemaphoreType.DMA
    student, right, left = pl.pallas_call(
        functools.partial(kernel, cfg),
        out_shape=(
            jax.ShapeDtypeStruct((rows, cols), BF16),
            jax.ShapeDtypeStruct((rrows, w), F32),
            jax.ShapeDtypeStruct((lrows, 2 * nb), F32),
        ),
        in_specs=[
            pl.BlockSpec(memory_space=pl.ANY),
            pl.BlockSpec(memory_space=pl.ANY),
            pl.BlockSpec(memory_space=V),
            pl.BlockSpec(memory_space=pl.ANY),
        ],
        out_specs=(
            pl.BlockSpec(memory_space=pl.ANY),
            pl.BlockSpec(memory_space=V),
            pl.BlockSpec(memory_space=V),
        ),
        scratch_shapes=[
            V((NC, tc, cols), BF16), V((NC, tc, cols), BF16), V((NC, tc, cols), BF16),
            V((NC, w, kl, tc), BF16), V((NC, B, cl, kl, tc), BF16),
            V((NC, nb, cl, tc), BF16), V((NC, B, kl, cl, tc), BF16),
            V((H, kl * w, 128), F32), V((H, cl * nb, 128), F32),
            V((S, rrows, w), BF16), V((S, lrows, w), BF16), V((lrows, w), F32), V((S, kl, r, w), F32), V((kl, w, w), BF16),
            V((nb, 128), F32), V((cl // 2, 128, 128), BF16), V((cl // 2, 128, 128), BF16),
            V((kl, w, w), F32), V((cl // 2 * nb, 128), F32), V((lrows, 128), F32), V((tc, tc), BF16),
            V((2, Q, rrows, w), BF16), V((Q, rrows, w), BF16), V((Q, rrows, w), BF16), V((Q, rrows, w), BF16),
            V((2, Q, lrows, w), BF16), V((Q, lrows, w), BF16), V((Q, lrows, w), BF16), V((Q, lrows, w), BF16),
            D((2, NC)), D((NC,)), D, D((Q - 1,)), D((Q - 1,)), D((Q,)), D((Q,)), D((Q - 1,)), D((Q - 1,)), D((Q,)), D((Q,)),
            D((NC, B - 1)), D((NC, B - 1)), D((NC,)), D((NC, B - 1)), D((NC, B - 1)), D((NC,)),
            D, D, D((Q - 1,)), D((Q - 1,)), D, D, D((Q - 1,)), D((Q - 1,)),
        ],
        compiler_params=pltpu.CompilerParams(
            collective_id=0, has_side_effects=True, vmem_limit_bytes=56 * 1024 * 1024),
        cost_estimate=pl.CostEstimate(
            flops=4 * 1024 * 1024 * 1024, bytes_accessed=3 * rows * cols * 2, transcendentals=rows * cols),
    )(tokens, right_factor.reshape(rrows, w), left_factor, target)
    steps = 4
    return pl.pallas_call(
        finish,
        grid=(steps,),
        out_shape=(
            jax.ShapeDtypeStruct((rows, cols), BF16),
            jax.ShapeDtypeStruct((kl, r, w), F32),
            jax.ShapeDtypeStruct((cl, lr, nb), F32),
        ),
        in_specs=[
            pl.BlockSpec((rows // steps, cols), lambda i: (i, 0)),
            pl.BlockSpec((rrows, w), lambda i: (0, 0)),
            pl.BlockSpec((lrows, 2 * nb), lambda i: (0, 0)),
        ],
        out_specs=(
            pl.BlockSpec((rows // steps, cols), lambda i: (i, 0)),
            pl.BlockSpec((kl, r, w), lambda i: (0, 0, 0)),
            pl.BlockSpec((cl, lr, nb), lambda i: (0, 0, 0)),
        ),
        compiler_params=pltpu.CompilerParams(vmem_limit_bytes=60 * 1024 * 1024),
        cost_estimate=pl.CostEstimate(flops=0, bytes_accessed=4 * rows * cols, transcendentals=0),
    )(student, right, left)


def solution(mesh):
    return jax.shard_map(
        functools.partial(shards, mesh.shape["seq"], mesh.shape["blk"]),
        mesh=mesh,
        in_specs=(P("seq", "blk"), P("blk", "seq", None), P("blk", "seq", None), P("seq", "blk")),
        out_specs=(P("seq", "blk"), P("blk", "seq", None), P("blk", "seq", None)),
        check_vma=False,
    )
```

```python
import functools
import math

import jax
import jax.numpy as jnp
from jax import lax
from jax.experimental import pallas as pl
from jax.experimental.pallas import tpu as pltpu
from jax.sharding import PartitionSpec as P

MESH = pl.DeviceIdType.MESH
F32 = jnp.float32
BF16 = jnp.bfloat16
C0 = math.sqrt(2.0 / math.pi)
NT = (((1,), (1,)), ((), ()))
NN = (((1,), (0,)), ((), ()))


def dot(a, b, dims):
    return lax.dot_general(a, b, dims, preferred_element_type=F32)


def partner(b, d, size):
    step, out = 1, b
    while step < size:
        if (d // step) % 2:
            out = out + step * (1 - 2 * ((b // step) % 2))
        step *= 2
    return out


def stack(parts):
    if parts[0].shape[0] % 16:
        return jnp.concatenate([v.astype(F32) for v in parts], axis=0).astype(BF16)
    return jnp.concatenate(parts, axis=0)


def eye(n):
    return (
        lax.broadcasted_iota(jnp.int32, (n, n), 0) == lax.broadcasted_iota(jnp.int32, (n, n), 1)
    ).astype(F32).astype(BF16)


def kernel(
    cfg, x_hbm, r_hbm, l_ref, t_hbm, st_hbm, rg_out, lg_out,
    xv, tv, stv, snd, recv, bsnd, brecv, fm, ft,
    gat, gatl, lfold, gf, rfull, lc, wb, wt, rg, lg, lga, idt,
    pbr, sibr, zsr, zrr, pbl, sibl, zsl, zrl,
    sx, sto, sf, gs, gr, fs, fr, hs, hr, is_, ir,
    as_, ar, al, bs, br, bl,
    rs1, rr1, rs2, rr2, ls1, lr1, ls2, lr2,
):
    S, B, NC, tc, kl, cl, nb, w, r, lr = cfg
    Q = S // 2
    H = tc // 128
    s = lax.axis_index("seq")
    b = lax.axis_index("blk")
    q, core = s // 2, s % 2
    scale = 1.0 / math.sqrt(float(S * NC * tc))
    rrows, lrows = kl * r, (cl // 2) * lr
    sib = (s + 1 - 2 * core, b)
    zpeers = [((((q + o) % Q) * 2 + core), b) for o in range(1, Q)]
    bids = [partner(b, d, B) for d in range(B - 1, 0, -1)]
    bpeers = [(s, i) for i in bids]

    def xload(j):
        return pltpu.make_async_copy(x_hbm.at[pl.ds(pl.multiple_of(j * tc, tc), tc)], xv.at[j], sx.at[0, j])

    def tload(j):
        return pltpu.make_async_copy(t_hbm.at[pl.ds(pl.multiple_of(j * tc, tc), tc)], tv.at[j], sx.at[1, j])

    def stout(j):
        return pltpu.make_async_copy(stv.at[j], st_hbm.at[pl.ds(pl.multiple_of(j * tc, tc), tc)], sto.at[j])

    own = pltpu.make_async_copy(r_hbm, gat.at[s], sf)
    own.start()
    for j in range(NC):
        xload(j).start()

    barrier = pltpu.get_barrier_semaphore()
    for peer in [sib] + zpeers + bpeers:
        pl.semaphore_signal(barrier, inc=1, device_id=peer, device_id_type=MESH)
    pl.semaphore_wait(barrier, 1 + len(zpeers) + len(bpeers))

    def spread(first, buf, ss, rs):
        return [
            pltpu.make_async_remote_copy(
                first, buf.at[s], ss.at[o], rs.at[o], device_id=zpeers[o], device_id_type=MESH)
            for o in range(Q - 1)
        ]

    def pass_on(first, buf, ss, rs):
        out = []
        for o in range(Q):
            src = ((q - o + Q) % Q) * 2 + core
            out.append(pltpu.make_async_remote_copy(
                buf.at[src] if o else first, buf.at[src], ss.at[o], rs.at[o],
                device_id=sib, device_id_type=MESH))
        return out

    gsend = spread(r_hbm, gat, gs, gr)
    fsend = pass_on(r_hbm, gat, fs, fr)
    for c in gsend:
        c.start()
    fsend[0].start()
    for j in range(NC):
        tload(j).start()
    idt[...] = eye(tc)
    rg[...] = jnp.zeros_like(rg)
    lg[...] = jnp.zeros_like(lg)
    for p in range(cl // 2):
        lfold[p * lr:(p + 1) * lr, :] = jnp.concatenate(
            [l_ref[2 * p].astype(F32), l_ref[2 * p + 1].astype(F32)], axis=1)
    gatl[s] = lfold[...].astype(BF16)
    own.wait()
    for o in range(1, Q):
        gsend[o - 1].wait_recv()
        fsend[o].start()
    hsend = spread(gatl.at[s], gatl, hs, hr)
    isend = pass_on(gatl.at[s], gatl, is_, ir)
    for c in hsend:
        c.start()
    isend[0].start()
    for o in range(Q):
        fsend[o].wait_recv()

    for i in range(S):
        gf[i] = gat[i].astype(F32).reshape(kl, r, w)

    def rbuild(k, _):
        rfull[k] = jnp.concatenate([gf[i, k] for i in range(S)], axis=0).astype(BF16)
        return 0

    lax.fori_loop(0, kl, rbuild, 0)

    def a_copy(j, d):
        return pltpu.make_async_remote_copy(
            snd.at[j, pl.ds(pl.multiple_of(bids[d] * cl, cl), cl)], recv.at[j, b],
            as_.at[j, d], ar.at[j, d], device_id=bpeers[d], device_id_type=MESH)

    def a_local(j):
        return pltpu.make_async_copy(
            snd.at[j, pl.ds(pl.multiple_of(b * cl, cl), cl)], recv.at[j, b], al.at[j])

    def forward(j, _):
        xload(j).wait()

        def mm(g, _):
            ks = [g * 4 + u for u in range(4)]
            res = [dot(rfull[k], xv[j, :, pl.ds(pl.multiple_of(k * w, w), w)], NT) for k in ks]
            for k, v in zip(ks, res):
                for h in range(H):
                    fm[h, pl.ds(pl.multiple_of(k * w, w), w), :] = v[:, h * 128:(h + 1) * 128]
            return 0

        lax.fori_loop(0, kl // 4, mm, 0)

        def turn(g, _):
            for u in range(8):
                c = g * 8 + u
                for h in range(H):
                    snd[j, c, :, h * 128:(h + 1) * 128] = fm[h, pl.ds(c, kl, stride=w), :].astype(BF16)
            return 0

        lax.fori_loop(0, w // 8, turn, 0)
        for d in range(B - 1):
            a_copy(j, d).start()
        a_local(j).start()
        return 0

    lax.fori_loop(0, NC, forward, 0)

    for o in range(1, Q):
        hsend[o - 1].wait_recv()
        isend[o].start()
    for o in range(Q):
        isend[o].wait_recv()

    gl = fm.at[0]
    lcols = lax.broadcasted_iota(jnp.int32, (nb, 128), 1)
    for i in range(S):
        gl[i * lrows:(i + 1) * lrows, :] = gatl[i].astype(F32)
    e128 = idt[:128, :128]

    def lbuild(p, _):
        for m in range(lr):
            lc[pl.ds(m, S, stride=lr), :] = gl[pl.ds(p * lr + m, S, stride=lrows), :]
        v = lc[...]
        both = jnp.concatenate(
            [jnp.where(lcols < nb, v, 0.0), jnp.where(lcols >= nb, v, 0.0)], axis=0).astype(BF16)
        wb[p] = both
        wt[p] = dot(e128, both, NT).astype(BF16)
        return 0

    lax.fori_loop(0, cl // 2, lbuild, 0)

    def b_copy(j, d):
        return pltpu.make_async_remote_copy(
            bsnd.at[j, pl.ds(pl.multiple_of(bids[d] * kl, kl), kl)], brecv.at[j, b],
            bs.at[j, d], br.at[j, d], device_id=bpeers[d], device_id_type=MESH)

    def b_local(j):
        return pltpu.make_async_copy(
            bsnd.at[j, pl.ds(pl.multiple_of(b * kl, kl), kl)], brecv.at[j, b], bl.at[j])

    def middle(j, _):
        tload(j).wait()
        a_local(j).wait()
        for d in range(B - 1):
            a_copy(j, d).wait_recv()

        def pairs(g, _):
            ps = [g * 4 + u for u in range(4)]
            cols = [pl.ds(pl.multiple_of(p * 128, 128), 128) for p in ps]
            tps = [stack([recv[j, a, 2 * p + c] for c in range(2) for a in range(B)]) for p in ps]
            vs = [dot(wb[p], tp, NN) for p, tp in zip(ps, tps)]
            tgts = [dot(e128, tv[j, :, c], NT) for c in cols]
            acts, pgs = [], []
            for v, tgt in zip(vs, tgts):
                v2 = v * v
                th = jnp.tanh(v * (C0 + (C0 * 0.044715) * v2))
                half = 0.5 + 0.5 * th
                act = v * half
                deriv = half + 0.5 * v * (1.0 - th * th) * (C0 + (3.0 * 0.044715 * C0) * v2)
                acts.append(act.astype(BF16))
                pgs.append((((act - tgt) * scale) * deriv).astype(BF16))
            tgs = [dot(wt[p], pg, NN) for p, pg in zip(ps, pgs)]
            sts = [dot(idt[...], act, NT).astype(BF16) for act in acts]
            fulls = [dot(pg, tp, NT) for pg, tp in zip(pgs, tps)]
            for p, tg in zip(ps, tgs):
                for h in range(H):
                    ft[h, pl.ds(pl.multiple_of(p * 128, 128), 128), :] = tg[:, h * 128:(h + 1) * 128]
            for c, st in zip(cols, sts):
                stv[j, :, c] = st
            for p, full in zip(ps, fulls):
                rows = pl.ds(pl.multiple_of(p * nb, nb), nb)
                lg[rows, :] += jnp.where(lcols < nb, full[:nb], full[nb:])
            return 0

        lax.fori_loop(0, cl // 8, pairs, 0)

        def turn(g, _):
            for u in range(4):
                k = g * 4 + u
                for h in range(H):
                    bsnd[j, k, :, h * 128:(h + 1) * 128] = ft[h, pl.ds(k, cl, stride=nb), :].astype(BF16)
            return 0

        lax.fori_loop(0, nb // 4, turn, 0)
        for d in range(B - 1):
            b_copy(j, d).start()
        b_local(j).start()
        stout(j).start()
        return 0

    lax.fori_loop(0, NC, middle, 0)

    l1 = pltpu.make_async_remote_copy(
        pbl.at[1 - core], sibl, ls1, lr1, device_id=sib, device_id_type=MESH)
    for i in range(S):
        for m in range(lr):
            lga[pl.ds(m, cl // 2, stride=lr), :] = lg[pl.ds(i * lr + m, cl // 2, stride=nb), :]
        pbl[i % 2, i // 2] = lga[...].astype(BF16)
    l1.start()

    def right(j, _):
        b_local(j).wait()
        for d in range(B - 1):
            b_copy(j, d).wait_recv()

        def blocks(g, _):
            ks = [g * 4 + u for u in range(4)]
            mgs = [stack([brecv[j, a, k] for a in range(B)]) for k in ks]
            res = [dot(mg, xv[j, :, pl.ds(pl.multiple_of(k * w, w), w)], NN) for k, mg in zip(ks, mgs)]
            for k, v in zip(ks, res):
                rg[k] += v
            return 0

        lax.fori_loop(0, kl // 4, blocks, 0)
        return 0

    def second(pb, sibv, zs, zr, ss, rs):
        for i in range(Q):
            zs[i] = (pb[core, i].astype(F32) + sibv[i].astype(F32)).astype(BF16)
        zr[q] = zs[q]
        copies = [
            pltpu.make_async_remote_copy(
                zs.at[(q + o + 1) % Q], zr.at[q], ss.at[o], rs.at[o],
                device_id=zpeers[o], device_id_type=MESH)
            for o in range(Q - 1)
        ]
        for c in copies:
            c.start()
        return copies

    def total(zr):
        acc = zr[0].astype(F32)
        for i in range(1, Q):
            acc = acc + zr[i].astype(F32)
        return acc

    right(0, 0)
    l1.wait_recv()
    l2 = second(pbl, sibl, zsl, zrl, ls2, lr2)
    lax.fori_loop(1, NC, right, 0)

    for i in range(S):
        pbr[i % 2, i // 2] = rg[:, i * r:(i + 1) * r, :].reshape(rrows, w).astype(BF16)
    r1 = pltpu.make_async_remote_copy(
        pbr.at[1 - core], sibr, rs1, rr1, device_id=sib, device_id_type=MESH)
    r1.start()
    for c in l2:
        c.wait_recv()
    lg_out[...] = total(zrl)
    r1.wait_recv()
    r2 = second(pbr, sibr, zsr, zrr, rs2, rr2)
    for c in gsend + fsend + hsend + isend + [l1, r1] + l2:
        c.wait_send()

    def drain(j, _):
        for d in range(B - 1):
            a_copy(j, d).wait_send()
            b_copy(j, d).wait_send()
        stout(j).wait()
        return 0

    lax.fori_loop(0, NC, drain, 0)
    for c in r2:
        c.wait_recv()
    rg_out[...] = total(zrr)
    for c in r2:
        c.wait_send()


def finish(st_ref, rg_ref, lg_ref, st_out, rg_out, lg_out):
    st_out[...] = st_ref[...]

    @pl.when(pl.program_id(0) == 0)
    def _():
        rg_out[...] = rg_ref[...].reshape(rg_out.shape)
        cl, lr, nb = lg_out.shape
        for p in range(cl // 2):
            v = lg_ref[p * lr:(p + 1) * lr, :]
            lg_out[2 * p] = v[:, :nb]
            lg_out[2 * p + 1] = v[:, nb:]


def shards(S, B, tokens, right_factor, left_factor, target):
    rows, cols = tokens.shape
    kl, r, w = right_factor.shape
    cl, lr, nb = left_factor.shape
    Q = S // 2
    NC = 4
    tc = rows // NC
    H = tc // 128
    rrows, lrows = kl * r, (cl // 2) * lr
    cfg = (S, B, NC, tc, kl, cl, nb, w, r, lr)
    V = pltpu.VMEM
    D = pltpu.SemaphoreType.DMA
    student, right, left = pl.pallas_call(
        functools.partial(kernel, cfg),
        out_shape=(
            jax.ShapeDtypeStruct((rows, cols), BF16),
            jax.ShapeDtypeStruct((rrows, w), F32),
            jax.ShapeDtypeStruct((lrows, 2 * nb), F32),
        ),
        in_specs=[
            pl.BlockSpec(memory_space=pl.ANY),
            pl.BlockSpec(memory_space=pl.ANY),
            pl.BlockSpec(memory_space=V),
            pl.BlockSpec(memory_space=pl.ANY),
        ],
        out_specs=(
            pl.BlockSpec(memory_space=pl.ANY),
            pl.BlockSpec(memory_space=V),
            pl.BlockSpec(memory_space=V),
        ),
        scratch_shapes=[
            V((NC, tc, cols), BF16), V((NC, tc, cols), BF16), V((NC, tc, cols), BF16),
            V((NC, w, kl, tc), BF16), V((NC, B, cl, kl, tc), BF16),
            V((NC, nb, cl, tc), BF16), V((NC, B, kl, cl, tc), BF16),
            V((H, kl * w, 128), F32), V((H, cl * nb, 128), F32),
            V((S, rrows, w), BF16), V((S, lrows, w), BF16), V((lrows, w), F32), V((S, kl, r, w), F32), V((kl, w, w), BF16),
            V((nb, 128), F32), V((cl // 2, 128, 128), BF16), V((cl // 2, 128, 128), BF16),
            V((kl, w, w), F32), V((cl // 2 * nb, 128), F32), V((lrows, 128), F32), V((tc, tc), BF16),
            V((2, Q, rrows, w), BF16), V((Q, rrows, w), BF16), V((Q, rrows, w), BF16), V((Q, rrows, w), BF16),
            V((2, Q, lrows, w), BF16), V((Q, lrows, w), BF16), V((Q, lrows, w), BF16), V((Q, lrows, w), BF16),
            D((2, NC)), D((NC,)), D, D((Q - 1,)), D((Q - 1,)), D((Q,)), D((Q,)), D((Q - 1,)), D((Q - 1,)), D((Q,)), D((Q,)),
            D((NC, B - 1)), D((NC, B - 1)), D((NC,)), D((NC, B - 1)), D((NC, B - 1)), D((NC,)),
            D, D, D((Q - 1,)), D((Q - 1,)), D, D, D((Q - 1,)), D((Q - 1,)),
        ],
        compiler_params=pltpu.CompilerParams(
            collective_id=0, has_side_effects=True, vmem_limit_bytes=56 * 1024 * 1024),
        cost_estimate=pl.CostEstimate(
            flops=4 * 1024 * 1024 * 1024, bytes_accessed=3 * rows * cols * 2, transcendentals=rows * cols),
    )(tokens, right_factor.reshape(rrows, w), left_factor, target)
    steps = 8
    return pl.pallas_call(
        finish,
        grid=(steps,),
        out_shape=(
            jax.ShapeDtypeStruct((rows, cols), BF16),
            jax.ShapeDtypeStruct((kl, r, w), F32),
            jax.ShapeDtypeStruct((cl, lr, nb), F32),
        ),
        in_specs=[
            pl.BlockSpec((rows // steps, cols), lambda i: (i, 0)),
            pl.BlockSpec((rrows, w), lambda i: (0, 0)),
            pl.BlockSpec((lrows, 2 * nb), lambda i: (0, 0)),
        ],
        out_specs=(
            pl.BlockSpec((rows // steps, cols), lambda i: (i, 0)),
            pl.BlockSpec((kl, r, w), lambda i: (0, 0, 0)),
            pl.BlockSpec((cl, lr, nb), lambda i: (0, 0, 0)),
        ),
        compiler_params=pltpu.CompilerParams(vmem_limit_bytes=60 * 1024 * 1024),
        cost_estimate=pl.CostEstimate(flops=0, bytes_accessed=4 * rows * cols, transcendentals=0),
    )(student, right, left)


def solution(mesh):
    return jax.shard_map(
        functools.partial(shards, mesh.shape["seq"], mesh.shape["blk"]),
        mesh=mesh,
        in_specs=(P("seq", "blk"), P("blk", "seq", None), P("blk", "seq", None), P("seq", "blk")),
        out_specs=(P("seq", "blk"), P("blk", "seq", None), P("blk", "seq", None)),
        check_vma=False,
    )
```

```python
import functools
import math

import jax
import jax.numpy as jnp
from jax import lax
from jax.experimental import pallas as pl
from jax.experimental.pallas import tpu as pltpu
from jax.sharding import PartitionSpec as P

MESH = pl.DeviceIdType.MESH
F32 = jnp.float32
BF16 = jnp.bfloat16
C0 = math.sqrt(2.0 / math.pi)
NT = (((1,), (1,)), ((), ()))
NN = (((1,), (0,)), ((), ()))


def dot(a, b, dims):
    return lax.dot_general(a, b, dims, preferred_element_type=F32)


def partner(b, d, size):
    step, out = 1, b
    while step < size:
        if (d // step) % 2:
            out = out + step * (1 - 2 * ((b // step) % 2))
        step *= 2
    return out


def stack(parts):
    if parts[0].shape[0] % 16:
        return jnp.concatenate([v.astype(F32) for v in parts], axis=0).astype(BF16)
    return jnp.concatenate(parts, axis=0)


def eye(n):
    return (
        lax.broadcasted_iota(jnp.int32, (n, n), 0) == lax.broadcasted_iota(jnp.int32, (n, n), 1)
    ).astype(F32).astype(BF16)


def kernel(
    cfg, x_hbm, r_hbm, l_ref, t_hbm, st_hbm, rg_out, lg_out,
    xv, tv, stv, snd, recv, bsnd, brecv, fm, ft,
    gat, gatl, lfold, gf, rfull, lc, wb, wt, rg, lg, lga, idt,
    pbr, sibr, zsr, zrr, pbl, sibl, zsl, zrl,
    sx, sto, sf, gs, gr, fs, fr, hs, hr, is_, ir,
    as_, ar, al, bs, br, bl,
    rs1, rr1, rs2, rr2, ls1, lr1, ls2, lr2,
):
    S, B, NC, tc, kl, cl, nb, w, r, lr = cfg
    Q = S // 2
    H = tc // 128
    s = lax.axis_index("seq")
    b = lax.axis_index("blk")
    q, core = s // 2, s % 2
    scale = 1.0 / math.sqrt(float(S * NC * tc))
    rrows, lrows = kl * r, (cl // 2) * lr
    sib = (s + 1 - 2 * core, b)
    zpeers = [((((q + o) % Q) * 2 + core), b) for o in range(1, Q)]
    bids = [partner(b, d, B) for d in range(B - 1, 0, -1)]
    bpeers = [(s, i) for i in bids]

    def xload(j):
        return pltpu.make_async_copy(x_hbm.at[pl.ds(pl.multiple_of(j * tc, tc), tc)], xv.at[j], sx.at[0, j])

    def tload(j):
        return pltpu.make_async_copy(t_hbm.at[pl.ds(pl.multiple_of(j * tc, tc), tc)], tv.at[j], sx.at[1, j])

    def stout(j):
        return pltpu.make_async_copy(stv.at[j], st_hbm.at[pl.ds(pl.multiple_of(j * tc, tc), tc)], sto.at[j])

    own = pltpu.make_async_copy(r_hbm, gat.at[s], sf)
    own.start()
    for j in range(NC):
        xload(j).start()

    barrier = pltpu.get_barrier_semaphore()
    for peer in [sib] + zpeers + bpeers:
        pl.semaphore_signal(barrier, inc=1, device_id=peer, device_id_type=MESH)
    pl.semaphore_wait(barrier, 1 + len(zpeers) + len(bpeers))

    def spread(first, buf, ss, rs):
        return [
            pltpu.make_async_remote_copy(
                first, buf.at[s], ss.at[o], rs.at[o], device_id=zpeers[o], device_id_type=MESH)
            for o in range(Q - 1)
        ]

    def pass_on(first, buf, ss, rs):
        out = []
        for o in range(Q):
            src = ((q - o + Q) % Q) * 2 + core
            out.append(pltpu.make_async_remote_copy(
                buf.at[src] if o else first, buf.at[src], ss.at[o], rs.at[o],
                device_id=sib, device_id_type=MESH))
        return out

    gsend = spread(r_hbm, gat, gs, gr)
    fsend = pass_on(r_hbm, gat, fs, fr)
    for c in gsend:
        c.start()
    fsend[0].start()
    for j in range(NC):
        tload(j).start()
    idt[...] = eye(tc)
    rg[...] = jnp.zeros_like(rg)
    lg[...] = jnp.zeros_like(lg)
    for p in range(cl // 2):
        lfold[p * lr:(p + 1) * lr, :] = jnp.concatenate(
            [l_ref[2 * p].astype(F32), l_ref[2 * p + 1].astype(F32)], axis=1)
    gatl[s] = lfold[...].astype(BF16)
    own.wait()
    for o in range(1, Q):
        gsend[o - 1].wait_recv()
        fsend[o].start()
    hsend = spread(gatl.at[s], gatl, hs, hr)
    isend = pass_on(gatl.at[s], gatl, is_, ir)
    for c in hsend:
        c.start()
    isend[0].start()
    for o in range(Q):
        fsend[o].wait_recv()

    for i in range(S):
        gf[i] = gat[i].astype(F32).reshape(kl, r, w)

    def rbuild(k, _):
        rfull[k] = jnp.concatenate([gf[i, k] for i in range(S)], axis=0).astype(BF16)
        return 0

    lax.fori_loop(0, kl, rbuild, 0)

    def a_copy(j, d):
        return pltpu.make_async_remote_copy(
            snd.at[j, pl.ds(pl.multiple_of(bids[d] * cl, cl), cl)], recv.at[j, b],
            as_.at[j, d], ar.at[j, d], device_id=bpeers[d], device_id_type=MESH)

    def a_local(j):
        return pltpu.make_async_copy(
            snd.at[j, pl.ds(pl.multiple_of(b * cl, cl), cl)], recv.at[j, b], al.at[j])

    def forward(j, _):
        xload(j).wait()

        def mm(g, _):
            ks = [g * 4 + u for u in range(4)]
            res = [dot(rfull[k], xv[j, :, pl.ds(pl.multiple_of(k * w, w), w)], NT) for k in ks]
            for k, v in zip(ks, res):
                for h in range(H):
                    fm[h, pl.ds(pl.multiple_of(k * w, w), w), :] = v[:, h * 128:(h + 1) * 128]
            return 0

        lax.fori_loop(0, kl // 4, mm, 0)

        def turn(g, _):
            for u in range(8):
                c = g * 8 + u
                for h in range(H):
                    snd[j, c, :, h * 128:(h + 1) * 128] = fm[h, pl.ds(c, kl, stride=w), :].astype(BF16)
            return 0

        lax.fori_loop(0, w // 8, turn, 0)
        a_local(j).start()
        return 0

    def launch(j, _):
        forward(j, 0)
        for d in range(B - 1):
            a_copy(j, d).start()
        return 0

    lax.fori_loop(0, 2, launch, 0)

    for o in range(1, Q):
        hsend[o - 1].wait_recv()
        isend[o].start()
    for o in range(Q):
        isend[o].wait_recv()

    gl = fm.at[0]
    lcols = lax.broadcasted_iota(jnp.int32, (nb, 128), 1)
    for i in range(S):
        gl[i * lrows:(i + 1) * lrows, :] = gatl[i].astype(F32)
    e128 = idt[:128, :128]

    def lbuild(p, _):
        for m in range(lr):
            lc[pl.ds(m, S, stride=lr), :] = gl[pl.ds(p * lr + m, S, stride=lrows), :]
        v = lc[...]
        block = jnp.concatenate(
            [jnp.where(lcols < nb, v, 0.0), jnp.where(lcols >= nb, v, 0.0)], axis=0).astype(BF16)
        wb[p] = block
        wt[p] = dot(e128, block, NT).astype(BF16)
        return 0

    lax.fori_loop(0, cl // 2, lbuild, 0)

    def b_copy(j, d):
        return pltpu.make_async_remote_copy(
            bsnd.at[j, pl.ds(pl.multiple_of(bids[d] * kl, kl), kl)], brecv.at[j, b],
            bs.at[j, d], br.at[j, d], device_id=bpeers[d], device_id_type=MESH)

    def b_local(j):
        return pltpu.make_async_copy(
            bsnd.at[j, pl.ds(pl.multiple_of(b * kl, kl), kl)], brecv.at[j, b], bl.at[j])

    def middle(j, _):
        tload(j).wait()
        a_local(j).wait()
        for d in range(B - 1):
            a_copy(j, d).wait_recv()

        def pairs(g, _):
            ps = [g * 4 + u for u in range(4)]
            cols = [pl.ds(pl.multiple_of(p * 128, 128), 128) for p in ps]
            tps = [stack([recv[j, a, 2 * p + c] for c in range(2) for a in range(B)]) for p in ps]
            vs = [dot(wb[p], tp, NN) for p, tp in zip(ps, tps)]
            tgts = [dot(e128, tv[j, :, c], NT) for c in cols]
            acts, pgs = [], []
            for v, tgt in zip(vs, tgts):
                v2 = v * v
                th = jnp.tanh(v * (C0 + (C0 * 0.044715) * v2))
                half = 0.5 + 0.5 * th
                act = v * half
                deriv = half + 0.5 * v * (1.0 - th * th) * (C0 + (3.0 * 0.044715 * C0) * v2)
                acts.append(act.astype(BF16))
                pgs.append((((act - tgt) * scale) * deriv).astype(BF16))
            tgs = [dot(wt[p], pg, NN) for p, pg in zip(ps, pgs)]
            sts = [dot(idt[...], act, NT).astype(BF16) for act in acts]
            fulls = [dot(pg, tp, NT) for pg, tp in zip(pgs, tps)]
            for p, tg in zip(ps, tgs):
                for h in range(H):
                    ft[h, pl.ds(pl.multiple_of(p * 128, 128), 128), :] = tg[:, h * 128:(h + 1) * 128]
            for c, st in zip(cols, sts):
                stv[j, :, c] = st
            for p, full in zip(ps, fulls):
                rows = pl.ds(pl.multiple_of(p * nb, nb), nb)
                lg[rows, :] += jnp.where(lcols < nb, full[:nb], full[nb:])
            return 0

        lax.fori_loop(0, cl // 8, pairs, 0)

        def turn(g, _):
            for u in range(4):
                k = g * 4 + u
                for h in range(H):
                    bsnd[j, k, :, h * 128:(h + 1) * 128] = ft[h, pl.ds(k, cl, stride=nb), :].astype(BF16)
            return 0

        lax.fori_loop(0, nb // 4, turn, 0)
        for d in range(B - 1):
            b_copy(j, d).start()
        b_local(j).start()
        stout(j).start()
        return 0

    def both(j, _):
        forward(j + 2, 0)
        for d in range(B - 1):
            a_copy(j, d).wait_send()
            a_copy(j + 2, d).start()
        return middle(j, 0)

    lax.fori_loop(0, NC - 2, both, 0)
    lax.fori_loop(NC - 2, NC, middle, 0)

    l1 = pltpu.make_async_remote_copy(
        pbl.at[1 - core], sibl, ls1, lr1, device_id=sib, device_id_type=MESH)
    for i in range(S):
        for m in range(lr):
            lga[pl.ds(m, cl // 2, stride=lr), :] = lg[pl.ds(i * lr + m, cl // 2, stride=nb), :]
        pbl[i % 2, i // 2] = lga[...].astype(BF16)
    l1.start()

    def right(j, _):
        b_local(j).wait()
        for d in range(B - 1):
            b_copy(j, d).wait_recv()

        def blocks(g, _):
            ks = [g * 4 + u for u in range(4)]
            mgs = [stack([brecv[j, a, k] for a in range(B)]) for k in ks]
            res = [dot(mg, xv[j, :, pl.ds(pl.multiple_of(k * w, w), w)], NN) for k, mg in zip(ks, mgs)]
            for k, v in zip(ks, res):
                rg[k] += v
            return 0

        lax.fori_loop(0, kl // 4, blocks, 0)
        return 0

    def second(pb, sibv, zs, zr, ss, rs):
        for i in range(Q):
            zs[i] = (pb[core, i].astype(F32) + sibv[i].astype(F32)).astype(BF16)
        zr[q] = zs[q]
        copies = [
            pltpu.make_async_remote_copy(
                zs.at[(q + o + 1) % Q], zr.at[q], ss.at[o], rs.at[o],
                device_id=zpeers[o], device_id_type=MESH)
            for o in range(Q - 1)
        ]
        for c in copies:
            c.start()
        return copies

    def total(zr):
        acc = zr[0].astype(F32)
        for i in range(1, Q):
            acc = acc + zr[i].astype(F32)
        return acc

    right(0, 0)
    l1.wait_recv()
    l2 = second(pbl, sibl, zsl, zrl, ls2, lr2)
    lax.fori_loop(1, NC, right, 0)

    for i in range(S):
        pbr[i % 2, i // 2] = rg[:, i * r:(i + 1) * r, :].reshape(rrows, w).astype(BF16)
    r1 = pltpu.make_async_remote_copy(
        pbr.at[1 - core], sibr, rs1, rr1, device_id=sib, device_id_type=MESH)
    r1.start()
    for c in l2:
        c.wait_recv()
    lg_out[...] = total(zrl)
    r1.wait_recv()
    r2 = second(pbr, sibr, zsr, zrr, rs2, rr2)
    for c in gsend + fsend + hsend + isend + [l1, r1] + l2:
        c.wait_send()

    def drain(j, _):
        for d in range(B - 1):
            b_copy(j, d).wait_send()
        stout(j).wait()
        return 0

    lax.fori_loop(0, NC, drain, 0)
    for j in (NC - 2, NC - 1):
        for d in range(B - 1):
            a_copy(j, d).wait_send()
    for c in r2:
        c.wait_recv()
    rg_out[...] = total(zrr)
    for c in r2:
        c.wait_send()


def finish(st_ref, rg_ref, lg_ref, st_out, rg_out, lg_out):
    st_out[...] = st_ref[...]

    @pl.when(pl.program_id(0) == 0)
    def _():
        rg_out[...] = rg_ref[...].reshape(rg_out.shape)
        cl, lr, nb = lg_out.shape
        for p in range(cl // 2):
            v = lg_ref[p * lr:(p + 1) * lr, :]
            lg_out[2 * p] = v[:, :nb]
            lg_out[2 * p + 1] = v[:, nb:]


def shards(S, B, tokens, right_factor, left_factor, target):
    rows, cols = tokens.shape
    kl, r, w = right_factor.shape
    cl, lr, nb = left_factor.shape
    Q = S // 2
    NC = 4
    tc = rows // NC
    H = tc // 128
    rrows, lrows = kl * r, (cl // 2) * lr
    cfg = (S, B, NC, tc, kl, cl, nb, w, r, lr)
    V = pltpu.VMEM
    D = pltpu.SemaphoreType.DMA
    student, right, left = pl.pallas_call(
        functools.partial(kernel, cfg),
        out_shape=(
            jax.ShapeDtypeStruct((rows, cols), BF16),
            jax.ShapeDtypeStruct((rrows, w), F32),
            jax.ShapeDtypeStruct((lrows, 2 * nb), F32),
        ),
        in_specs=[
            pl.BlockSpec(memory_space=pl.ANY),
            pl.BlockSpec(memory_space=pl.ANY),
            pl.BlockSpec(memory_space=V),
            pl.BlockSpec(memory_space=pl.ANY),
        ],
        out_specs=(
            pl.BlockSpec(memory_space=pl.ANY),
            pl.BlockSpec(memory_space=V),
            pl.BlockSpec(memory_space=V),
        ),
        scratch_shapes=[
            V((NC, tc, cols), BF16), V((NC, tc, cols), BF16), V((NC, tc, cols), BF16),
            V((NC, w, kl, tc), BF16), V((NC, B, cl, kl, tc), BF16),
            V((NC, nb, cl, tc), BF16), V((NC, B, kl, cl, tc), BF16),
            V((H, kl * w, 128), F32), V((H, cl * nb, 128), F32),
            V((S, rrows, w), BF16), V((S, lrows, w), BF16), V((lrows, w), F32), V((S, kl, r, w), F32), V((kl, w, w), BF16),
            V((nb, 128), F32), V((cl // 2, 128, 128), BF16), V((cl // 2, 128, 128), BF16),
            V((kl, w, w), F32), V((cl // 2 * nb, 128), F32), V((lrows, 128), F32), V((tc, tc), BF16),
            V((2, Q, rrows, w), BF16), V((Q, rrows, w), BF16), V((Q, rrows, w), BF16), V((Q, rrows, w), BF16),
            V((2, Q, lrows, w), BF16), V((Q, lrows, w), BF16), V((Q, lrows, w), BF16), V((Q, lrows, w), BF16),
            D((2, NC)), D((NC,)), D, D((Q - 1,)), D((Q - 1,)), D((Q,)), D((Q,)), D((Q - 1,)), D((Q - 1,)), D((Q,)), D((Q,)),
            D((NC, B - 1)), D((NC, B - 1)), D((NC,)), D((NC, B - 1)), D((NC, B - 1)), D((NC,)),
            D, D, D((Q - 1,)), D((Q - 1,)), D, D, D((Q - 1,)), D((Q - 1,)),
        ],
        compiler_params=pltpu.CompilerParams(
            collective_id=0, has_side_effects=True, vmem_limit_bytes=56 * 1024 * 1024),
        cost_estimate=pl.CostEstimate(
            flops=4 * 1024 * 1024 * 1024, bytes_accessed=3 * rows * cols * 2, transcendentals=rows * cols),
    )(tokens, right_factor.reshape(rrows, w), left_factor, target)
    steps = 4
    return pl.pallas_call(
        finish,
        grid=(steps,),
        out_shape=(
            jax.ShapeDtypeStruct((rows, cols), BF16),
            jax.ShapeDtypeStruct((kl, r, w), F32),
            jax.ShapeDtypeStruct((cl, lr, nb), F32),
        ),
        in_specs=[
            pl.BlockSpec((rows // steps, cols), lambda i: (i, 0)),
            pl.BlockSpec((rrows, w), lambda i: (0, 0)),
            pl.BlockSpec((lrows, 2 * nb), lambda i: (0, 0)),
        ],
        out_specs=(
            pl.BlockSpec((rows // steps, cols), lambda i: (i, 0)),
            pl.BlockSpec((kl, r, w), lambda i: (0, 0, 0)),
            pl.BlockSpec((cl, lr, nb), lambda i: (0, 0, 0)),
        ),
        compiler_params=pltpu.CompilerParams(vmem_limit_bytes=60 * 1024 * 1024),
        cost_estimate=pl.CostEstimate(flops=0, bytes_accessed=4 * rows * cols, transcendentals=0),
    )(student, right, left)


def solution(mesh):
    return jax.shard_map(
        functools.partial(shards, mesh.shape["seq"], mesh.shape["blk"]),
        mesh=mesh,
        in_specs=(P("seq", "blk"), P("blk", "seq", None), P("blk", "seq", None), P("seq", "blk")),
        out_specs=(P("seq", "blk"), P("blk", "seq", None), P("blk", "seq", None)),
        check_vma=False,
    )
```
